32 devices in a mesh: groups: 2 (over y), fsdp: 8 (over z, x), dp: 2 (over core).
Axes of the slice: x: 2, y: 2, z: 4, core: 2. Of those that a mesh axis runs over, the one named last changes fastest.
Arguments:
- acts: bfloat16 [2, 32, 128, 14336], P(None, ('groups', 'fsdp', 'dp')), parts along dimension 1, may hold values from -48 to 48
- grads_out: bfloat16 [2, 32, 128, 4096], P(None, ('groups', 'fsdp', 'dp')), parts along dimension 1, may hold values from -48 to 48
- basis_in: bfloat16 [2, 14336, 64], P(None, 'fsdp'), may hold values from -0.046875 to 0.046875
- basis_out: bfloat16 [2, 4096, 64], P(None, 'fsdp'), may hold values from -0.09375 to 0.09375
- query_codes: bfloat16 [1024, 8192], P(('fsdp', 'dp')), may hold values from -6 to 6
Outputs:
- scores: float32 [32, 1024], P(('groups', 'fsdp', 'dp')), parts along dimension 0
The draws below stay inside these ranges and needn't reach their ends.
There are 2 independent parts, one for each index of `groups`. The reference program is written for one: setup_inputs(seed, part) draws one part's arguments, and reference() takes and returns one part's arrays. A program takes and returns all parts, laid end to end along the dimension named above; an argument that names none is the same for every part. Nothing has to cross between parts.
All inputs are finite; a program needn't handle non-finite values.
Results may differ from the reference program's by a relative error of at most 0.0003.
Values may be sent and summed in bfloat16 or wider, within the bound.
A program may use at most 128 MiB of HBM per device.

```python
import math
import jax
import jax.numpy as jnp
from jax import lax

D = 4096
FF = 14336
R = 64
LAYERS = 2
LENGTH = 128
QUERIES = 1024
EXAMPLES = 16


def textured(key, shape, spread):
    keys = jax.random.split(key, 5)
    layers, examples, length, features = shape
    gauss = jax.random.normal(keys[0], shape, jnp.float32)
    half_log = 0.5 * math.log(spread)
    column_scale = jnp.exp(jax.random.uniform(keys[3], (layers, 1, 1, features), jnp.float32, minval=-half_log, maxval=half_log))
    row_scale = jnp.exp(jax.random.uniform(keys[4], (layers, examples, length, 1), jnp.float32, minval=-half_log, maxval=half_log))
    token_position = jnp.arange(examples, dtype=jnp.float32) / max(examples - 1, 1)
    ramp = jnp.exp(math.log(3.0) * (token_position - 0.5)).reshape(1, examples, 1, 1)
    values = gauss * column_scale * row_scale * ramp
    return jnp.clip(values, -48.0, 48.0).astype(jnp.bfloat16)


def draw_acts(key, part):
    key = jax.random.fold_in(key, 11)
    return textured(key, (LAYERS, EXAMPLES, LENGTH, FF), 10.0)


def draw_grads_out(key, part):
    key = jax.random.fold_in(key, 12)
    return textured(key, (LAYERS, EXAMPLES, LENGTH, D), 10.0)


def levels(key, dims, pieces, low, high):
    def one(dim, parts):
        heights = jax.random.uniform(jax.random.fold_in(jax.random.fold_in(key, 6), dim), (parts,), jnp.float32, low / len(pieces), high / len(pieces))
        return jnp.repeat(jnp.exp(heights), dims[dim] // parts).reshape((-1,) + (1,) * (len(dims) - dim - 1))

    factor_of = one(*pieces[0])
    for cut in pieces[1:]:
        factor_of = factor_of * one(*cut)
    return factor_of


def gaussian(key, dims, scale, reach, cuts=(), kind=jnp.bfloat16):
    array = jax.random.normal(key, dims, jnp.float32) * scale
    if len(cuts) > 0:
        array = levels(key, dims, cuts, -0.22, 0.18) * array
    return jnp.clip(array, min=-reach, max=reach).astype(kind)


def setup_inputs(seed: int = 0, part: int = 0) -> dict:
    splits = jax.random.split(jax.random.key(seed), 6)
    part_keys = jax.random.split(jax.random.fold_in(splits[5], part), 6)
    acts = draw_acts(jax.random.fold_in(jax.random.fold_in(splits[5], part), 71), part)
    grads_out = draw_grads_out(jax.random.fold_in(jax.random.fold_in(splits[5], part), 71), part)
    basis_in = gaussian(splits[2], (LAYERS, FF, R), FF ** -0.5, 0.046875, ((1, 8),))
    basis_out = gaussian(splits[3], (LAYERS, D, R), D ** -0.5, 0.09375, ((1, 8),))
    query_codes = gaussian(splits[4], (QUERIES, LAYERS * R * R), 1.0, 6.0, ((0, 16),))
    return {"acts": acts, "grads_out": grads_out, "basis_in": basis_in, "basis_out": basis_out, "query_codes": query_codes}


def damped_inverse(covariance, samples):
    averaged = covariance / samples
    ridge_term = 0.1 * jnp.trace(averaged) / averaged.shape[0]
    identity_matrix = jnp.eye(averaged.shape[0], dtype=averaged.dtype)
    factor = jnp.linalg.cholesky(averaged + ridge_term * identity_matrix)
    return jax.scipy.linalg.cho_solve((factor, True), identity_matrix)

def reference(acts, grads_out, basis_in, basis_out, query_codes):

    def project(example):
        inputs = lax.dynamic_index_in_dim(acts, example, 1, keepdims=False)
        outputs = lax.dynamic_index_in_dim(grads_out, example, 1, keepdims=False)
        projected_in = jnp.stack([jnp.dot(inputs[which_layer].astype(jnp.float32), basis_in[which_layer].astype(jnp.float32), preferred_element_type=jnp.float32) for which_layer in range(LAYERS)])
        projected_out = jnp.stack([jnp.dot(outputs[which_layer].astype(jnp.float32), basis_out[which_layer].astype(jnp.float32), preferred_element_type=jnp.float32) for which_layer in range(LAYERS)])
        return (projected_in, projected_out)
    projected_in, projected_out = lax.map(project, jnp.arange(EXAMPLES, dtype=jnp.int32))
    highest_precision = lax.Precision.HIGHEST
    gradient_codes = jnp.einsum('elti,eltj->elij', projected_in, projected_out, precision=highest_precision)
    covariance_in = jnp.einsum('elti,eltj->lij', projected_in, projected_in, precision=highest_precision)
    covariance_out = jnp.einsum('elti,eltj->lij', projected_out, projected_out, precision=highest_precision)
    samples = float(EXAMPLES * LENGTH)
    inverse_in = jax.vmap(damped_inverse, in_axes=(0, None))(covariance_in, samples)
    output_inverse = jax.vmap(damped_inverse, in_axes=(0, None))(covariance_out, samples)
    preconditioned_codes = jnp.einsum('lij,eljk->elik', inverse_in, gradient_codes, precision=highest_precision)
    preconditioned_codes = jnp.einsum('bzpo,zoc->bzpc', preconditioned_codes, output_inverse, precision=highest_precision)
    flattened = preconditioned_codes.reshape(EXAMPLES, LAYERS * R * R)
    queries = query_codes.astype(jnp.float32)
    scores = lax.dot_general(flattened, queries, (((1,), (1,)), ((), ())), precision=highest_precision)
    return scores * (1.0 / math.sqrt(LAYERS * R * R * LENGTH))
```

```python
import functools
import math

import jax
import jax.numpy as jnp
from jax import lax
from jax.experimental import pallas as pl
from jax.experimental.pallas import tpu as pltpu
from jax.sharding import PartitionSpec as P

MESH = pl.DeviceIdType.MESH
HIGHEST = lax.Precision.HIGHEST
F32 = jnp.float32


def dot(a, b, ca, cb, precision=None):
    return lax.dot_general(
        a, b, (((ca,), (cb,)), ((), ())), precision=precision, preferred_element_type=F32
    )


def invert_all(mats):
    n = mats[0].shape[0]
    rows = lax.broadcasted_iota(jnp.int32, (n, n), 0)
    lanes = lax.broadcasted_iota(jnp.int32, (n, n), 1)
    lane1 = lax.broadcasted_iota(jnp.int32, (1, n), 1)
    unit = jnp.where(rows == lanes, 1.0, 0.0).astype(F32)
    mats = list(mats)
    for k in range(n):
        for m, a in enumerate(mats):
            recip = 1.0 / a[k : k + 1, k : k + 1]
            col = a[:, k : k + 1]
            row = jnp.where(lane1 == k, 1.0, a[k : k + 1, :]) * recip
            cleared = jnp.where(lanes == k, unit, a)
            mats[m] = jnp.where(rows == k, row, cleared - col * row)
    return mats


def kernel(
    nf, nc, scale,
    acts_hbm, grads_hbm, basis_in, basis_out, query_hbm, out_ref,
    acts, grads, queries, win, wout, acc, arrived, codes, cond, flat, stage, landed,
    load_sem, bs_send, bs_recv, cov_send, cov_recv, g_send, g_recv, s_send, s_recv,
):
    f, c = lax.axis_index("fsdp"), lax.axis_index("dp")
    n = nf * nc
    bits = n.bit_length() - 1
    me = f * nc + c
    length = nf // 2
    z, x = f // 2, f % 2
    r = basis_in.shape[2]
    tokens = acts.shape[0] // 2

    loads = [
        pltpu.make_async_copy(src, dst, load_sem.at[i])
        for i, (src, dst) in enumerate(((grads_hbm, grads), (acts_hbm, acts), (query_hbm, queries)))
    ]
    for load in loads:
        load.start()

    def peer(rank):
        return {"fsdp": rank // nc, "dp": rank % nc}

    barrier = pltpu.get_barrier_semaphore()

    def greet(d, _):
        pl.semaphore_signal(barrier, inc=1, device_id=peer((me + d) % n), device_id_type=MESH)
        return _

    lax.fori_loop(1, n, greet, 0)

    kinds = ((win, basis_in), (wout, basis_out))
    for full, mine in kinds:
        rows = mine.shape[1]
        full[pl.ds(pl.multiple_of(f * rows, rows), rows), :] = jnp.concatenate(
            [mine[0], mine[1]], axis=1
        )
    pl.semaphore_wait(barrier, n - 1)

    def piece(kind, owner, half):
        full, mine = kinds[kind]
        rows = mine.shape[1] // 2
        return full.at[pl.ds(pl.multiple_of((owner * 2 + half) * rows, rows), rows), :]

    def hop(kind, owner, way):
        target = (f - 2, f + 2, f + 1 - 2 * x, f)[way]
        core = 1 - c if way == 3 else c
        return pltpu.make_async_remote_copy(
            src_ref=piece(kind, owner, c),
            dst_ref=piece(kind, owner, c),
            send_sem=bs_send.at[kind, way, owner],
            recv_sem=bs_recv.at[kind, owner, c],
            device_id={"fsdp": target, "dp": core},
            device_id_type=MESH,
        )

    def came(kind, owner, half):
        ref = piece(kind, owner, half)
        return pltpu.make_async_copy(ref, ref, bs_recv.at[kind, owner, half])

    def each(fn, *args):
        for kind in (0, 1):
            fn(kind, *args)

    def when(cond_, fn, *args):
        pl.when(cond_)(lambda: each(fn, *args))

    def go(kind, owner, way):
        hop(kind, owner, way).start()

    def sent(kind, owner, way):
        hop(kind, owner, way).wait_send()

    def arrive(kind, owner, half):
        came(kind, owner, half).wait()

    each(go, f, 2)
    when(z > 0, go, f, 0)
    when(z < length - 1, go, f, 1)

    def step(k, _):
        for low, way in ((True, 1), (False, 0)):
            owner = f - 2 * k if low else f + 2 * k
            there = z >= k if low else z + k < length
            onward = there & (z < length - 1 if low else z > 0)

            @pl.when(there)
            def _():
                for kind in (0, 1):
                    arrive(kind, owner, c)
                    go(kind, owner, 2)
                    go(kind, owner, 3)

            when(onward, go, owner, way)
        return _

    def from_pair(k, _):
        base = f + 1 - 2 * x
        for low in (True, False):
            owner = base - 2 * k if low else base + 2 * k
            there = z >= k if low else z + k < length

            @pl.when(there)
            def _():
                for kind in (0, 1):
                    arrive(kind, owner, c)
                    go(kind, owner, 3)
        return _

    partner = f + 1 - 2 * x
    for k in range(1, length):
        step(k, 0)
        if k == 1:
            each(arrive, partner, c)
            each(go, partner, 3)
        else:
            from_pair(k - 1, 0)
    if length > 1:
        from_pair(length - 1, 0)
    else:
        each(arrive, partner, c)
        each(go, partner, 3)

    def others(d, _):
        owner = (f + d) % nf
        each(arrive, owner, 1 - c)
        return _

    lax.fori_loop(1, nf, others, 0)
    for load in loads:
        load.wait()

    lane = lax.broadcasted_iota(jnp.int32, (1, 2 * r), 1)
    first = lane < r

    def project(source, full):
        width = source.shape[1]
        chunk = 2048 if width % 2048 == 0 else width

        def part(i, total):
            at = pl.ds(pl.multiple_of(i * chunk, chunk), chunk)
            return total + dot(source[:, at], full[at, :], 1, 0)

        both = lax.fori_loop(
            0, width // chunk, part, jnp.zeros((source.shape[0], 2 * r), F32)
        )
        return jnp.where(first, both[:tokens], both[tokens:])

    def packed(both):
        return jnp.where(first, both[:r], both[r:])

    p_out = project(grads, wout)
    p_in = project(acts, win)
    acc[0, :r, :] = packed(dot(p_in, p_in, 0, 0, HIGHEST))
    acc[0, r:, :] = packed(dot(p_out, p_out, 0, 0, HIGHEST))

    place = 0
    for b in range(bits):
        place = place + (me // (1 << b)) % 2 * (1 << (bits - 1 - b))

    def partner_of(t):
        b = bits - 1 - t
        return me + (1 - 2 * ((me // (1 << b)) % 2)) * (1 << b)

    def cov_copy(t):
        return pltpu.make_async_remote_copy(
            src_ref=acc.at[t], dst_ref=arrived.at[t], send_sem=cov_send.at[t],
            recv_sem=cov_recv.at[t], device_id=peer(partner_of(t)), device_id_type=MESH,
        )

    def code_copy(t):
        size = 1 << t
        at = pl.ds(place // size * size, size)
        return pltpu.make_async_remote_copy(
            src_ref=codes.at[at], dst_ref=codes.at[at], send_sem=g_send.at[t],
            recv_sem=g_recv.at[t], device_id=peer(partner_of(t)), device_id_type=MESH,
        )

    def code_wait(t):
        size = 1 << t
        code_copy(t).wait_send()
        sib = place // size
        sib = sib + 1 - 2 * (sib % 2)
        ref = codes.at[pl.ds(sib * size, size)]
        pltpu.make_async_copy(ref, ref, g_recv.at[t]).wait()

    for t in range(bits):
        cov_copy(t).start()
        if t == 0:
            codes[place] = packed(dot(p_in, p_out, 0, 0, HIGHEST))
            code_copy(0).start()
        cov_copy(t).wait()
        acc[t + 1] = acc[t] + arrived[t]
        if t >= 1:
            code_wait(t - 1)
            code_copy(t).start()

    samples = float(n * tokens)
    eye = (
        lax.broadcasted_iota(jnp.int32, (r, r), 0) == lax.broadcasted_iota(jnp.int32, (r, r), 1)
    )
    mats = []
    for side in (0, 1):
        for layer in (0, 1):
            a = acc[bits, side * r : (side + 1) * r, :][:, layer * r : (layer + 1) * r] / samples
            diag = jnp.where(eye, a, 0.0)
            trace = jnp.sum(jnp.sum(diag, axis=1, keepdims=True), axis=0, keepdims=True)
            mats.append(a + jnp.where(eye, 0.1 * trace / r, 0.0))
    in0, in1, out0, out1 = invert_all(mats)
    code_wait(bits - 1)

    left = jnp.concatenate([in0, in1], axis=0)
    none = jnp.zeros((r, r), F32)
    right = jnp.concatenate(
        [jnp.concatenate([out0, none], axis=1), jnp.concatenate([none, out1], axis=1)], axis=0
    )

    for e in range(n):
        mid = packed(dot(left, codes[e], 1, 0, HIGHEST))
        cond[e * r : (e + 1) * r, :] = mid
    cond[...] = dot(cond[...], right, 1, 0, HIGHEST) * scale

    half = r * r
    for k in range(r // 2):
        a = cond[pl.ds(2 * k, n, stride=r), :]
        b = cond[pl.ds(2 * k + 1, n, stride=r), :]
        flat[:, k * 2 * r : (k + 1) * 2 * r] = jnp.where(first, a, pltpu.roll(b, r, 1))
        flat[:, half + k * 2 * r : half + (k + 1) * 2 * r] = jnp.where(first, pltpu.roll(a, r, 1), b)
    whole = flat[...]
    high = whole.astype(jnp.bfloat16)
    low = (whole - high.astype(F32)).astype(jnp.bfloat16)
    scores = dot(high, queries[...], 1, 1) + dot(low, queries[...], 1, 1)
    wide = stage.shape[2]
    q = scores.shape[1]
    if q < wide:
        scores = jnp.concatenate([scores, jnp.zeros((n, wide - q), F32)], axis=1)
    stage[...] = jnp.broadcast_to(scores[:, None, :], stage.shape)

    def reverse(p):
        return int(format(p, "b").zfill(bits)[::-1], 2)

    def score_copy(p):
        return pltpu.make_async_remote_copy(
            src_ref=stage.at[p], dst_ref=landed.at[me], send_sem=s_send.at[p],
            recv_sem=s_recv.at[me], device_id=peer(reverse(p)), device_id_type=MESH,
        )

    for p in range(n):
        pl.when(place != p)(lambda p=p: score_copy(p).start())
    landed[me] = stage[place]

    each(sent, f, 2)
    when(z > 0, sent, f, 0)
    when(z < length - 1, sent, f, 1)
    for k in range(1, length):
        for low_side, way in ((True, 1), (False, 0)):
            owner = f - 2 * k if low_side else f + 2 * k
            there = z >= k if low_side else z + k < length
            onward = there & (z < length - 1 if low_side else z > 0)
            when(there, sent, owner, 2)
            when(onward, sent, owner, way)

    def other_sent(d, _):
        each(sent, (f + d) % nf, 3)
        return _

    lax.fori_loop(1, nf, other_sent, 0)
    for p in range(n):
        pl.when(place != p)(lambda p=p: score_copy(p).wait_send())

    def score_in(d, _):
        who = (me + d) % n
        ref = landed.at[who]
        pltpu.make_async_copy(ref, ref, s_recv.at[who]).wait()
        return _

    lax.fori_loop(1, n, score_in, 0)
    out_ref[...] = landed[:, 0, :q]


def solution(mesh):
    nf, nc = mesh.shape["fsdp"], mesh.shape["dp"]
    n = nf * nc
    bits = n.bit_length() - 1

    def on_device(acts, grads_out, basis_in, basis_out, query_codes):
        layers, _, length, ff = acts.shape
        width = grads_out.shape[3]
        r = basis_in.shape[2]
        q, code_width = query_codes.shape
        bf16 = jnp.bfloat16
        scale = 1.0 / math.sqrt(code_width * length)
        vmem, anywhere = pl.BlockSpec(memory_space=pltpu.VMEM), pl.BlockSpec(memory_space=pl.ANY)
        dma = pltpu.SemaphoreType.DMA
        lanes = -(-q // 128) * 128
        scores = pl.pallas_call(
            functools.partial(kernel, nf, nc, scale),
            out_shape=jax.ShapeDtypeStruct((n, q), F32),
            in_specs=[anywhere, anywhere, vmem, vmem, anywhere],
            out_specs=vmem,
            scratch_shapes=[
                pltpu.VMEM((layers * length, ff), bf16),
                pltpu.VMEM((layers * length, width), bf16),
                pltpu.VMEM((q, code_width), bf16),
                pltpu.VMEM((ff, layers * r), bf16),
                pltpu.VMEM((width, layers * r), bf16),
                pltpu.VMEM((bits + 1, 2 * r, 2 * r), F32),
                pltpu.VMEM((bits, 2 * r, 2 * r), F32),
                pltpu.VMEM((n, r, 2 * r), F32),
                pltpu.VMEM((n * r, 2 * r), F32),
                pltpu.VMEM((n, code_width), F32),
                pltpu.VMEM((n, 8, lanes), F32),
                pltpu.VMEM((n, 8, lanes), F32),
                dma((3,)),
                dma((2, 4, nf)),
                dma((2, nf, 2)),
                dma((bits,)),
                dma((bits,)),
                dma((bits,)),
                dma((bits,)),
                dma((n,)),
                dma((n,)),
            ],
            compiler_params=pltpu.CompilerParams(
                collective_id=0, has_side_effects=True, vmem_limit_bytes=56 * 1024 * 1024
            ),
        )(
            acts.reshape(layers * length, ff),
            grads_out.reshape(layers * length, width),
            basis_in,
            basis_out,
            query_codes,
        )
        return scores.reshape(1, n * q)

    rows = P(None, ("groups", "fsdp", "dp"), None, None)
    return jax.shard_map(
        on_device,
        mesh=mesh,
        in_specs=(rows, rows, P(None, "fsdp", None), P(None, "fsdp", None), P(("fsdp", "dp"), None)),
        out_specs=P(("groups", "fsdp", "dp"), None),
        check_vma=False,
    )
```

```python
import functools
import math

import jax
import jax.numpy as jnp
from jax import lax
from jax.experimental import pallas as pl
from jax.experimental.pallas import tpu as pltpu
from jax.sharding import PartitionSpec as P

MESH = pl.DeviceIdType.MESH
HIGHEST = lax.Precision.HIGHEST
F32 = jnp.float32


def dot(a, b, ca, cb, precision=None):
    return lax.dot_general(
        a, b, (((ca,), (cb,)), ((), ())), precision=precision, preferred_element_type=F32
    )


def invert_all(mats):
    n = mats[0].shape[0]
    rows = lax.broadcasted_iota(jnp.int32, (n, n), 0)
    lanes = lax.broadcasted_iota(jnp.int32, (n, n), 1)
    lane1 = lax.broadcasted_iota(jnp.int32, (1, n), 1)
    unit = jnp.where(rows == lanes, 1.0, 0.0).astype(F32)
    mats = list(mats)
    for k in range(n):
        for m, a in enumerate(mats):
            recip = 1.0 / a[k : k + 1, k : k + 1]
            col = a[:, k : k + 1]
            row = jnp.where(lane1 == k, 1.0, a[k : k + 1, :]) * recip
            cleared = jnp.where(lanes == k, unit, a)
            mats[m] = jnp.where(rows == k, row, cleared - col * row)
    return mats


def kernel(
    nf, nc, scale,
    acts_hbm, grads_hbm, basis_in, basis_out, query_hbm, out_ref,
    acts, grads, queries, win, wout, sum_in, sum_out, acc, arrived, codes, cond, flat, stage, landed,
    load_sem, bs_send, bs_recv, cov_send, cov_recv, g_send, g_recv, s_send, s_recv,
):
    f, c, g = lax.axis_index("fsdp"), lax.axis_index("dp"), lax.axis_index("groups")
    n = nf * nc
    bits = n.bit_length() - 1
    me = f * nc + c
    length = nf // 2
    z, x = f // 2, f % 2
    r = basis_in.shape[0] // 2
    tokens = acts.shape[0] // 2

    loads = [
        pltpu.make_async_copy(src, dst, load_sem.at[i])
        for i, (src, dst) in enumerate(((grads_hbm, grads), (acts_hbm, acts), (query_hbm, queries)))
    ]
    for load in loads:
        load.start()

    def peer(rank):
        return {"fsdp": rank // nc, "dp": rank % nc}

    barrier = pltpu.get_barrier_semaphore()

    def greet(d, _):
        pl.semaphore_signal(barrier, inc=1, device_id=peer((me + d) % n), device_id_type=MESH)
        return _

    lax.fori_loop(1, n, greet, 0)
    other_group = {"groups": 1 - g, "fsdp": f, "dp": c}
    pl.semaphore_signal(barrier, inc=1, device_id=other_group, device_id_type=MESH)

    kinds = ((win, basis_in, acts, sum_in), (wout, basis_out, grads, sum_out))
    for full, mine, _, total in kinds:
        full[f] = mine[...]
    pl.semaphore_wait(barrier, n)

    def piece(kind, owner, half, part=None):
        full = kinds[kind][0]
        if part is None:
            return full.at[owner, pl.ds(pl.multiple_of(half * r, r), r), :]
        start = pl.multiple_of(half * r + part * (r // 2), r // 2)
        return full.at[owner, pl.ds(start, r // 2), :]

    def hop(kind, owner, way, halved=False):
        target = f + 1 - 2 * x if way == 2 else {0: f - 2, 1: f + 2}.get(way, f)
        part = None
        if way in (2, 5) or (way == 3 and halved):
            part = g
        elif way == 4:
            part = 1 - g
        ref = piece(kind, owner, c, part)
        return pltpu.make_async_remote_copy(
            src_ref=ref,
            dst_ref=ref,
            send_sem=bs_send.at[kind, way, owner],
            recv_sem=bs_recv.at[kind, owner, c, 0 if part is None else part],
            device_id={
                "groups": 1 - g if way == 5 else g,
                "fsdp": target,
                "dp": 1 - c if way in (3, 4) else c,
            },
            device_id_type=MESH,
        )

    def each(fn, *args):
        for kind in (0, 1):
            fn(kind, *args)

    def when(cond_, fn, *args):
        pl.when(cond_)(lambda: each(fn, *args))

    def go(kind, owner, way, halved=False):
        hop(kind, owner, way, halved).start()

    def sent(kind, owner, way, halved=False):
        hop(kind, owner, way, halved).wait_send()

    def arrive(kind, owner, half, part=None):
        ref = piece(kind, owner, half, part)
        sem = bs_recv.at[kind, owner, half, 0 if part is None else part]
        pltpu.make_async_copy(ref, ref, sem).wait()

    early = all(mine.shape[1] % 128 == 0 for _, mine, _, _ in kinds)

    def multiply(kind, owner):
        full, mine, source, total = kinds[kind]
        rows = mine.shape[1]
        start = owner * rows
        if not isinstance(owner, int):
            start = pl.multiple_of(start, rows)
        total[...] += dot(source[:, pl.ds(start, rows)], full[owner], 1, 1)

    def on_line(kind, owner):
        arrive(kind, owner, 1 - c)
        if early:
            multiply(kind, owner)

    def on_pair(kind, owner):
        arrive(kind, owner, 1 - c, 0)
        arrive(kind, owner, 1 - c, 1)
        if early:
            multiply(kind, owner)

    def from_line(kind, owner):
        arrive(kind, owner, c)
        go(kind, owner, 2)
        go(kind, owner, 3)

    def from_pair(kind, owner):
        arrive(kind, owner, c, g)
        go(kind, owner, 5)
        go(kind, owner, 3, True)

    def from_group(kind, owner):
        arrive(kind, owner, c, 1 - g)
        go(kind, owner, 4)

    def sides(fn, base, k):
        if k == 0:
            each(fn, base)
        elif 0 < k < length:
            when(z >= k, fn, base - 2 * k)
            when(z + k < length, fn, base + 2 * k)

    def onward(fn, k):
        if k == 0:
            when(z > 0, fn, f, 0)
            when(z < length - 1, fn, f, 1)
        elif k < length:
            when((z >= k) & (z < length - 1), fn, f - 2 * k, 1)
            when((z + k < length) & (z > 0), fn, f + 2 * k, 0)

    def pass_on(k):
        if k >= length:
            return
        for there, owner, way, further in (
            (z >= k, f - 2 * k, 1, z < length - 1),
            (z + k < length, f + 2 * k, 0, z > 0),
        ):
            @pl.when(there)
            def _():
                for kind in (0, 1):
                    arrive(kind, owner, c)
                    pl.when(further)(lambda kind=kind: go(kind, owner, way))
                    go(kind, owner, 2)
                    go(kind, owner, 3)

    partner = f + 1 - 2 * x
    onward(go, 0)
    each(go, f, 2)
    for _, _, _, total in kinds:
        total[...] = jnp.zeros_like(total)
    for load in loads:
        load.wait()
    if early:
        each(multiply, f)
    for k in range(1, length + 3):
        pass_on(k)
        sides(from_pair, partner, k - 1)
        if k >= 2:
            sides(from_group, partner, k - 2)
            if k > 2:
                sides(on_line, f, k - 2)
        if k >= 3:
            sides(on_pair, partner, k - 3)
    if not early:
        for owner in range(nf):
            each(multiply, owner)

    lane = lax.broadcasted_iota(jnp.int32, (1, 2 * r), 1)
    first = lane < r

    def packed(both):
        return jnp.where(first, both[:r], both[r:])

    p_out = jnp.where(first, sum_out[:tokens, :], sum_out[tokens:, :])
    p_in = jnp.where(first, sum_in[:tokens, :], sum_in[tokens:, :])
    acc[0, :r, :] = packed(dot(p_in, p_in, 0, 0, HIGHEST))
    acc[0, r:, :] = packed(dot(p_out, p_out, 0, 0, HIGHEST))

    place = 0
    for b in range(bits):
        place = place + (me // (1 << b)) % 2 * (1 << (bits - 1 - b))

    def partner_of(t):
        b = bits - 1 - t
        return me + (1 - 2 * ((me // (1 << b)) % 2)) * (1 << b)

    def cov_copy(t):
        return pltpu.make_async_remote_copy(
            src_ref=acc.at[t], dst_ref=arrived.at[t], send_sem=cov_send.at[t],
            recv_sem=cov_recv.at[t], device_id=peer(partner_of(t)), device_id_type=MESH,
        )

    def code_copy(t):
        size = 1 << t
        at = pl.ds(place // size * size, size)
        return pltpu.make_async_remote_copy(
            src_ref=codes.at[at], dst_ref=codes.at[at], send_sem=g_send.at[t],
            recv_sem=g_recv.at[t], device_id=peer(partner_of(t)), device_id_type=MESH,
        )

    def code_wait(t):
        size = 1 << t
        code_copy(t).wait_send()
        sib = place // size
        sib = sib + 1 - 2 * (sib % 2)
        ref = codes.at[pl.ds(sib * size, size)]
        pltpu.make_async_copy(ref, ref, g_recv.at[t]).wait()

    for t in range(bits):
        cov_copy(t).start()
        if t == 0:
            codes[place] = packed(dot(p_in, p_out, 0, 0, HIGHEST))
            code_copy(0).start()
        cov_copy(t).wait()
        acc[t + 1] = acc[t] + arrived[t]
        if t >= 1:
            code_wait(t - 1)
            code_copy(t).start()

    samples = float(n * tokens)
    eye = (
        lax.broadcasted_iota(jnp.int32, (r, r), 0) == lax.broadcasted_iota(jnp.int32, (r, r), 1)
    )
    mats = []
    for side in (0, 1):
        for layer in (0, 1):
            a = acc[bits, side * r : (side + 1) * r, :][:, layer * r : (layer + 1) * r] / samples
            diag = jnp.where(eye, a, 0.0)
            trace = jnp.sum(jnp.sum(diag, axis=1, keepdims=True), axis=0, keepdims=True)
            mats.append(a + jnp.where(eye, 0.1 * trace / r, 0.0))
    in0, in1, out0, out1 = invert_all(mats)
    code_wait(bits - 1)

    left = jnp.concatenate([in0, in1], axis=0)
    none = jnp.zeros((r, r), F32)
    right = jnp.concatenate(
        [jnp.concatenate([out0, none], axis=1), jnp.concatenate([none, out1], axis=1)], axis=0
    )

    for e in range(n):
        mid = packed(dot(left, codes[e], 1, 0, HIGHEST))
        cond[e * r : (e + 1) * r, :] = mid
    cond[...] = dot(cond[...], right, 1, 0, HIGHEST) * scale

    half = r * r
    for k in range(r // 2):
        a = cond[pl.ds(2 * k, n, stride=r), :]
        b = cond[pl.ds(2 * k + 1, n, stride=r), :]
        flat[:, k * 2 * r : (k + 1) * 2 * r] = jnp.where(first, a, pltpu.roll(b, r, 1))
        flat[:, half + k * 2 * r : half + (k + 1) * 2 * r] = jnp.where(first, pltpu.roll(a, r, 1), b)
    whole = flat[...]
    high = whole.astype(jnp.bfloat16)
    low = (whole - high.astype(F32)).astype(jnp.bfloat16)
    scores = dot(high, queries[...], 1, 1) + dot(low, queries[...], 1, 1)
    wide = stage.shape[2]
    q = scores.shape[1]
    if q < wide:
        scores = jnp.concatenate([scores, jnp.zeros((n, wide - q), F32)], axis=1)
    stage[...] = jnp.broadcast_to(scores[:, None, :], stage.shape)

    def reverse(p):
        return int(format(p, "b").zfill(bits)[::-1], 2)

    def score_copy(p):
        return pltpu.make_async_remote_copy(
            src_ref=stage.at[p], dst_ref=landed.at[me], send_sem=s_send.at[p],
            recv_sem=s_recv.at[me], device_id=peer(reverse(p)), device_id_type=MESH,
        )

    for p in range(n):
        pl.when(place != p)(lambda p=p: score_copy(p).start())
    landed[me] = stage[place]

    for k in range(length):
        onward(sent, k)
        sides(lambda kind, owner: sent(kind, owner, 2), f, k)
        if k > 0:
            sides(lambda kind, owner: sent(kind, owner, 3), f, k)
        for way in (5, 3, 4):
            sides(lambda kind, owner: sent(kind, owner, way, way == 3), partner, k)
    for p in range(n):
        pl.when(place != p)(lambda p=p: score_copy(p).wait_send())

    def score_in(d, _):
        who = (me + d) % n
        ref = landed.at[who]
        pltpu.make_async_copy(ref, ref, s_recv.at[who]).wait()
        return _

    lax.fori_loop(1, n, score_in, 0)
    out_ref[...] = landed[:, 0, :q]


def solution(mesh):
    nf, nc = mesh.shape["fsdp"], mesh.shape["dp"]
    n = nf * nc
    bits = n.bit_length() - 1

    def on_device(acts, grads_out, basis_in, basis_out, query_codes):
        layers, _, length, ff = acts.shape
        width = grads_out.shape[3]
        r = basis_in.shape[2]
        q, code_width = query_codes.shape
        bf16 = jnp.bfloat16
        scale = 1.0 / math.sqrt(code_width * length)
        vmem, anywhere = pl.BlockSpec(memory_space=pltpu.VMEM), pl.BlockSpec(memory_space=pl.ANY)
        dma = pltpu.SemaphoreType.DMA
        lanes = -(-q // 128) * 128
        scores = pl.pallas_call(
            functools.partial(kernel, nf, nc, scale),
            out_shape=jax.ShapeDtypeStruct((n, q), F32),
            in_specs=[anywhere, anywhere, vmem, vmem, anywhere],
            out_specs=vmem,
            scratch_shapes=[
                pltpu.VMEM((layers * length, ff), bf16),
                pltpu.VMEM((layers * length, width), bf16),
                pltpu.VMEM((q, code_width), bf16),
                pltpu.VMEM((nf, layers * r, basis_in.shape[1]), bf16),
                pltpu.VMEM((nf, layers * r, basis_out.shape[1]), bf16),
                pltpu.VMEM((layers * length, layers * r), F32),
                pltpu.VMEM((layers * length, layers * r), F32),
                pltpu.VMEM((bits + 1, 2 * r, 2 * r), F32),
                pltpu.VMEM((bits, 2 * r, 2 * r), F32),
                pltpu.VMEM((n, r, 2 * r), F32),
                pltpu.VMEM((n * r, 2 * r), F32),
                pltpu.VMEM((n, code_width), F32),
                pltpu.VMEM((n, 8, lanes), F32),
                pltpu.VMEM((n, 8, lanes), F32),
                dma((3,)),
                dma((2, 6, nf)),
                dma((2, nf, 2, 2)),
                dma((bits,)),
                dma((bits,)),
                dma((bits,)),
                dma((bits,)),
                dma((n,)),
                dma((n,)),
            ],
            compiler_params=pltpu.CompilerParams(
                collective_id=0, has_side_effects=True, vmem_limit_bytes=56 * 1024 * 1024
            ),
        )(
            acts.reshape(layers * length, ff),
            grads_out.reshape(layers * length, width),
            basis_in.transpose(0, 2, 1).reshape(layers * r, -1),
            basis_out.transpose(0, 2, 1).reshape(layers * r, -1),
            query_codes,
        )
        return scores.reshape(1, n * q)

    rows = P(None, ("groups", "fsdp", "dp"), None, None)
    return jax.shard_map(
        on_device,
        mesh=mesh,
        in_specs=(rows, rows, P(None, "fsdp", None), P(None, "fsdp", None), P(("fsdp", "dp"), None)),
        out_specs=P(("groups", "fsdp", "dp"), None),
        check_vma=False,
    )
```

```python
import functools
import math

import jax
import jax.numpy as jnp
from jax import lax
from jax.experimental import pallas as pl
from jax.experimental.pallas import tpu as pltpu
from jax.sharding import PartitionSpec as P

MESH = pl.DeviceIdType.MESH
HIGHEST = lax.Precision.HIGHEST
F32 = jnp.float32


def dot(a, b, ca, cb, precision=None):
    return lax.dot_general(
        a, b, (((ca,), (cb,)), ((), ())), precision=precision, preferred_element_type=F32
    )


def invert_all(mats):
    n = mats[0].shape[0]
    rows = lax.broadcasted_iota(jnp.int32, (n, n), 0)
    lanes = lax.broadcasted_iota(jnp.int32, (n, n), 1)
    lane1 = lax.broadcasted_iota(jnp.int32, (1, n), 1)
    unit = jnp.where(rows == lanes, 1.0, 0.0).astype(F32)
    mats = list(mats)
    for k in range(n):
        for m, a in enumerate(mats):
            recip = 1.0 / a[k : k + 1, k : k + 1]
            col = a[:, k : k + 1]
            row = jnp.where(lane1 == k, 1.0, a[k : k + 1, :]) * recip
            cleared = jnp.where(lanes == k, unit, a)
            mats[m] = jnp.where(rows == k, row, cleared - col * row)
    return mats


def kernel(
    nf, nc, scale,
    acts_hbm, grads_hbm, basis_in, basis_out, query_hbm, out_ref,
    acts, grads, queries, win, wout, sum_in, sum_out, acc, arrived, codes, cond, flat, stage, landed,
    load_sem, bs_send, bs_recv, cov_send, cov_recv, g_send, g_recv, s_send, s_recv,
):
    f, c, g = lax.axis_index("fsdp"), lax.axis_index("dp"), lax.axis_index("groups")
    n = nf * nc
    bits = n.bit_length() - 1
    me = f * nc + c
    length = nf // 2
    z, x = f // 2, f % 2
    r = basis_in.shape[0] // 2
    tokens = acts.shape[0] // 2

    loads = [
        pltpu.make_async_copy(src, dst, load_sem.at[i])
        for i, (src, dst) in enumerate(((grads_hbm, grads), (acts_hbm, acts), (query_hbm, queries)))
    ]
    for load in loads:
        load.start()

    def peer(rank):
        return {"fsdp": rank // nc, "dp": rank % nc}

    barrier = pltpu.get_barrier_semaphore()

    def greet(d, _):
        pl.semaphore_signal(barrier, inc=1, device_id=peer((me + d) % n), device_id_type=MESH)
        return _

    lax.fori_loop(1, n, greet, 0)
    other_group = {"groups": 1 - g, "fsdp": f, "dp": c}
    pl.semaphore_signal(barrier, inc=1, device_id=other_group, device_id_type=MESH)

    kinds = ((win, basis_in, acts, sum_in), (wout, basis_out, grads, sum_out))
    for full, mine, _, total in kinds:
        full[f] = mine[...]
    pl.semaphore_wait(barrier, n)

    def piece(kind, owner, half, part=None):
        full = kinds[kind][0]
        if part is None:
            return full.at[owner, pl.ds(pl.multiple_of(half * r, r), r), :]
        start = pl.multiple_of(half * r + part * (r // 2), r // 2)
        return full.at[owner, pl.ds(start, r // 2), :]

    def hop(kind, owner, way, halved=False):
        target = f + 1 - 2 * x if way == 2 else {0: f - 2, 1: f + 2}.get(way, f)
        part = None
        if way in (2, 5) or (way == 3 and halved):
            part = g
        elif way == 4:
            part = 1 - g
        ref = piece(kind, owner, c, part)
        return pltpu.make_async_remote_copy(
            src_ref=ref,
            dst_ref=ref,
            send_sem=bs_send.at[kind, way, owner],
            recv_sem=bs_recv.at[kind, owner, c, 0 if part is None else part],
            device_id={
                "groups": 1 - g if way == 5 else g,
                "fsdp": target,
                "dp": 1 - c if way in (3, 4) else c,
            },
            device_id_type=MESH,
        )

    def each(fn, *args):
        for kind in (0, 1):
            fn(kind, *args)

    def when(cond_, fn, *args):
        pl.when(cond_)(lambda: each(fn, *args))

    def go(kind, owner, way, halved=False):
        hop(kind, owner, way, halved).start()

    def sent(kind, owner, way, halved=False):
        hop(kind, owner, way, halved).wait_send()

    def arrive(kind, owner, half, part=None):
        ref = piece(kind, owner, half, part)
        sem = bs_recv.at[kind, owner, half, 0 if part is None else part]
        pltpu.make_async_copy(ref, ref, sem).wait()

    early = all(mine.shape[1] % 128 == 0 for _, mine, _, _ in kinds)

    def multiply(kind, owner):
        full, mine, source, total = kinds[kind]
        rows = mine.shape[1]
        start = owner * rows
        if not isinstance(owner, int):
            start = pl.multiple_of(start, rows)
        total[...] += dot(source[:, pl.ds(start, rows)], full[owner], 1, 1)

    def on_line(kind, owner):
        arrive(kind, owner, 1 - c)
        if early:
            multiply(kind, owner)

    def on_pair(kind, owner):
        arrive(kind, owner, 1 - c, 0)
        arrive(kind, owner, 1 - c, 1)
        if early:
            multiply(kind, owner)

    def from_line(kind, owner):
        arrive(kind, owner, c)
        go(kind, owner, 2)
        go(kind, owner, 3)

    def from_pair(kind, owner):
        arrive(kind, owner, c, g)
        go(kind, owner, 5)
        go(kind, owner, 3, True)

    def from_group(kind, owner):
        arrive(kind, owner, c, 1 - g)
        go(kind, owner, 4)

    def sides(fn, base, k):
        if k == 0:
            each(fn, base)
        elif 0 < k < length:
            when(z >= k, fn, base - 2 * k)
            when(z + k < length, fn, base + 2 * k)

    def onward(fn, k):
        if k == 0:
            when(z > 0, fn, f, 0)
            when(z < length - 1, fn, f, 1)
        elif k < length:
            when((z >= k) & (z < length - 1), fn, f - 2 * k, 1)
            when((z + k < length) & (z > 0), fn, f + 2 * k, 0)

    def pass_on(k):
        if k >= length:
            return
        for there, owner, way, further in (
            (z >= k, f - 2 * k, 1, z < length - 1),
            (z + k < length, f + 2 * k, 0, z > 0),
        ):
            @pl.when(there)
            def _():
                for kind in (0, 1):
                    arrive(kind, owner, c)
                    pl.when(further)(lambda kind=kind: go(kind, owner, way))
                    go(kind, owner, 2)
                    go(kind, owner, 3)

    partner = f + 1 - 2 * x
    onward(go, 0)
    each(go, f, 2)
    for _, _, _, total in kinds:
        total[...] = jnp.zeros_like(total)
    for load in loads[:2]:
        load.wait()
    if early:
        each(multiply, f)
    for k in range(1, length + 3):
        pass_on(k)
        sides(from_pair, partner, k - 1)
        if k >= 2:
            sides(from_group, partner, k - 2)
            if k > 2:
                sides(on_line, f, k - 2)
        if k >= 3:
            sides(on_pair, partner, k - 3)
    if not early:
        for owner in range(nf):
            each(multiply, owner)

    lane = lax.broadcasted_iota(jnp.int32, (1, 2 * r), 1)
    first = lane < r

    def packed(both):
        return jnp.where(first, both[:r], both[r:])

    p_out = jnp.where(first, sum_out[:tokens, :], sum_out[tokens:, :])
    p_in = jnp.where(first, sum_in[:tokens, :], sum_in[tokens:, :])
    acc[0, :r, :] = packed(dot(p_in, p_in, 0, 0, HIGHEST))
    acc[0, r:, :] = packed(dot(p_out, p_out, 0, 0, HIGHEST))

    place = 0
    for b in range(bits):
        place = place + (me // (1 << b)) % 2 * (1 << (bits - 1 - b))

    def partner_of(t):
        b = bits - 1 - t
        return me + (1 - 2 * ((me // (1 << b)) % 2)) * (1 << b)

    own_side = pl.ds(pl.multiple_of(c * r, r), r)

    def cov_copy(t):
        if t == 0:
            src, dst, to = acc.at[0], arrived.at[0], me + 1 - 2 * c
        elif t == bits:
            src = acc.at[bits, own_side, :]
            dst, to = src, me + 1 - 2 * c
        else:
            src, dst, to = acc.at[t, own_side, :], arrived.at[t, own_side, :], partner_of(t - 1)
        return pltpu.make_async_remote_copy(
            src_ref=src, dst_ref=dst, send_sem=cov_send.at[t],
            recv_sem=cov_recv.at[t], device_id=peer(to), device_id_type=MESH,
        )

    def code_copy(t):
        size = 1 << t
        at = pl.ds(place // size * size, size)
        return pltpu.make_async_remote_copy(
            src_ref=codes.at[at], dst_ref=codes.at[at], send_sem=g_send.at[t],
            recv_sem=g_recv.at[t], device_id=peer(partner_of(t)), device_id_type=MESH,
        )

    def code_wait(t):
        size = 1 << t
        code_copy(t).wait_send()
        sib = place // size
        sib = sib + 1 - 2 * (sib % 2)
        ref = codes.at[pl.ds(sib * size, size)]
        pltpu.make_async_copy(ref, ref, g_recv.at[t]).wait()

    for t in range(bits):
        cov_copy(t).start()
        if t == 0:
            codes[place] = packed(dot(p_in, p_out, 0, 0, HIGHEST))
            code_copy(0).start()
        cov_copy(t).wait()
        if t == 0:
            acc[1] = acc[0] + arrived[0]
        else:
            acc[t + 1, own_side, :] = acc[t, own_side, :] + arrived[t, own_side, :]
        if t >= 1:
            code_wait(t - 1)
            code_copy(t).start()

    cov_copy(bits).start()
    cov_copy(bits).wait_send()
    other_side = acc.at[bits, pl.ds(pl.multiple_of((1 - c) * r, r), r), :]
    pltpu.make_async_copy(other_side, other_side, cov_recv.at[bits]).wait()

    samples = float(n * tokens)
    eye = (
        lax.broadcasted_iota(jnp.int32, (r, r), 0) == lax.broadcasted_iota(jnp.int32, (r, r), 1)
    )
    mats = []
    for side in (0, 1):
        for layer in (0, 1):
            a = acc[bits, side * r : (side + 1) * r, :][:, layer * r : (layer + 1) * r] / samples
            diag = jnp.where(eye, a, 0.0)
            trace = jnp.sum(jnp.sum(diag, axis=1, keepdims=True), axis=0, keepdims=True)
            mats.append(a + jnp.where(eye, 0.1 * trace / r, 0.0))
    in0, in1, out0, out1 = invert_all(mats)
    code_wait(bits - 1)

    left = jnp.concatenate([in0, in1], axis=0)
    none = jnp.zeros((r, r), F32)
    right = jnp.concatenate(
        [jnp.concatenate([out0, none], axis=1), jnp.concatenate([none, out1], axis=1)], axis=0
    )

    for e in range(n):
        mid = packed(dot(left, codes[e], 1, 0, HIGHEST))
        cond[e * r : (e + 1) * r, :] = mid
    cond[...] = dot(cond[...], right, 1, 0, HIGHEST) * scale

    half = r * r
    for k in range(r // 2):
        a = cond[pl.ds(2 * k, n, stride=r), :]
        b = cond[pl.ds(2 * k + 1, n, stride=r), :]
        flat[:, k * 2 * r : (k + 1) * 2 * r] = jnp.where(first, a, pltpu.roll(b, r, 1))
        flat[:, half + k * 2 * r : half + (k + 1) * 2 * r] = jnp.where(first, pltpu.roll(a, r, 1), b)
    loads[2].wait()
    whole = flat[...]
    high = whole.astype(jnp.bfloat16)
    low = (whole - high.astype(F32)).astype(jnp.bfloat16)
    scores = dot(high, queries[...], 1, 1) + dot(low, queries[...], 1, 1)
    wide = stage.shape[2]
    q = scores.shape[1]
    if q < wide:
        scores = jnp.concatenate([scores, jnp.zeros((n, wide - q), F32)], axis=1)
    stage[...] = jnp.broadcast_to(scores[:, None, :], stage.shape)

    def reverse(p):
        return int(format(p, "b").zfill(bits)[::-1], 2)

    def score_copy(p):
        return pltpu.make_async_remote_copy(
            src_ref=stage.at[p], dst_ref=landed.at[me], send_sem=s_send.at[p],
            recv_sem=s_recv.at[me], device_id=peer(reverse(p)), device_id_type=MESH,
        )

    for p in range(n):
        pl.when(place != p)(lambda p=p: score_copy(p).start())
    landed[me] = stage[place]

    for k in range(length):
        onward(sent, k)
        sides(lambda kind, owner: sent(kind, owner, 2), f, k)
        if k > 0:
            sides(lambda kind, owner: sent(kind, owner, 3), f, k)
        for way in (5, 3, 4):
            sides(lambda kind, owner: sent(kind, owner, way, way == 3), partner, k)
    for p in range(n):
        pl.when(place != p)(lambda p=p: score_copy(p).wait_send())

    def score_in(d, _):
        who = (me + d) % n
        ref = landed.at[who]
        pltpu.make_async_copy(ref, ref, s_recv.at[who]).wait()
        return _

    lax.fori_loop(1, n, score_in, 0)
    out_ref[...] = landed[:, 0, :q]


def solution(mesh):
    nf, nc = mesh.shape["fsdp"], mesh.shape["dp"]
    n = nf * nc
    bits = n.bit_length() - 1

    def on_device(acts, grads_out, basis_in, basis_out, query_codes):
        layers, _, length, ff = acts.shape
        width = grads_out.shape[3]
        r = basis_in.shape[2]
        q, code_width = query_codes.shape
        bf16 = jnp.bfloat16
        scale = 1.0 / math.sqrt(code_width * length)
        vmem, anywhere = pl.BlockSpec(memory_space=pltpu.VMEM), pl.BlockSpec(memory_space=pl.ANY)
        dma = pltpu.SemaphoreType.DMA
        lanes = -(-q // 128) * 128
        scores = pl.pallas_call(
            functools.partial(kernel, nf, nc, scale),
            out_shape=jax.ShapeDtypeStruct((n, q), F32),
            in_specs=[anywhere, anywhere, vmem, vmem, anywhere],
            out_specs=vmem,
            scratch_shapes=[
                pltpu.VMEM((layers * length, ff), bf16),
                pltpu.VMEM((layers * length, width), bf16),
                pltpu.VMEM((q, code_width), bf16),
                pltpu.VMEM((nf, layers * r, basis_in.shape[1]), bf16),
                pltpu.VMEM((nf, layers * r, basis_out.shape[1]), bf16),
                pltpu.VMEM((layers * length, layers * r), F32),
                pltpu.VMEM((layers * length, layers * r), F32),
                pltpu.VMEM((bits + 1, 2 * r, 2 * r), F32),
                pltpu.VMEM((bits, 2 * r, 2 * r), F32),
                pltpu.VMEM((n, r, 2 * r), F32),
                pltpu.VMEM((n * r, 2 * r), F32),
                pltpu.VMEM((n, code_width), F32),
                pltpu.VMEM((n, 8, lanes), F32),
                pltpu.VMEM((n, 8, lanes), F32),
                dma((3,)),
                dma((2, 6, nf)),
                dma((2, nf, 2, 2)),
                dma((bits + 1,)),
                dma((bits + 1,)),
                dma((bits,)),
                dma((bits,)),
                dma((n,)),
                dma((n,)),
            ],
            compiler_params=pltpu.CompilerParams(
                collective_id=0, has_side_effects=True, vmem_limit_bytes=56 * 1024 * 1024
            ),
        )(
            acts.reshape(layers * length, ff),
            grads_out.reshape(layers * length, width),
            basis_in.transpose(0, 2, 1).reshape(layers * r, -1),
            basis_out.transpose(0, 2, 1).reshape(layers * r, -1),
            query_codes,
        )
        return scores.reshape(1, n * q)

    rows = P(None, ("groups", "fsdp", "dp"), None, None)
    return jax.shard_map(
        on_device,
        mesh=mesh,
        in_specs=(rows, rows, P(None, "fsdp", None), P(None, "fsdp", None), P(("fsdp", "dp"), None)),
        out_specs=P(("groups", "fsdp", "dp"), None),
        check_vma=False,
    )
```
